768 devices in a mesh: space: 96 (over z, x, core), member: 8 (over y).
Axes of the slice: x: 4, y: 8, z: 12, core: 2. Of those that a mesh axis runs over, the one named last changes fastest.
Arguments:
- coarse_vertex_embedding: bfloat16 [8, 3072, 1024], P('member', 'space'), may hold values from -6 to 6
- lattice_bypass_embedding: bfloat16 [8, 12288, 1024], P('member', 'space'), may hold values from -6 to 6
- initial_condition: float32 [8, 12288, 100], P('member', 'space'), may hold values from -6 to 6
- verifying_analysis: float32 [12288, 100], P('space'), may hold values from -8 to 8
- edge_index: int32 [12288, 3], P('space'), may hold values from 0 to 95
- area_weight: float32 [12288], P('space'), may hold values from 0.4 to 4
- variable_weight: float32 [100], replicated, may hold values from 0.2 to 2
- query_weight: bfloat16 [1024, 1024], replicated, may hold values from -2 to 2
- keyval_weight: bfloat16 [1024, 2048], replicated, may hold values from -0.1875 to 0.1875
- output_weight: bfloat16 [1024, 1024], replicated, may hold values from -0.1875 to 0.1875
- output_channel_matrix: bfloat16 [1024, 100], replicated, may hold values from -0.1875 to 0.1875
Outputs:
- grad_mesh: bfloat16 [8, 3072, 1024], P('member', 'space')
- grad_grid: bfloat16 [8, 12288, 1024], P('member', 'space')
- probabilistic_penalty: float32 [12288, 100], P(('space', 'member'))
The draws below stay inside these ranges and needn't reach their ends.
Inputs may be any that keep to these rules, and one draw needn't show every extreme that they name: `edge_index`: node numbers 0 to 31 name nodes of the previous longitude sector, the next 32 the grid point's own sector, the last 32 the following sector; sectors wrap around the globe.
All inputs are finite; a program needn't handle non-finite values.
Results may differ from the reference program's by a relative error of at most 0.03.
Values may be sent and summed in bfloat16 or wider, within the bound.
No kernel may reach another device: no remote copies, remote signals or barrier semaphores. Data moves between devices by JAX's collectives and lax.ppermute only.
A program may use at most 64 MiB of HBM per device.

```python
import math
import jax
import jax.numpy as jnp
from jax import lax

C = 1024
HEADS = 16
V = 100
EDGES = 3
GRID_DEV = 128
MESH_DEV = 32
REALISATION_TOTAL = 8
GRID = 12288
NODES = 3072
N_SPACE = 96


def set_ends(drawn, key, low, largest):
    shape = drawn.shape
    index_at = [jax.random.randint(jax.random.fold_in(key, axis), (), 0, shape[axis]) for axis in range(len(shape))]
    drawn = drawn.at[tuple(index_at)].set(low)
    longest = shape.index(max(shape))
    index_at[longest] = (index_at[longest] + 1) % shape[longest]
    return drawn.at[tuple(index_at)].set(largest)


def steps_of(rng, dims, cuts, low, largest):
    gain, own = 1.0, jax.random.fold_in(rng, 6)
    for axis_at, blocks in cuts:
        draws = jnp.exp(jax.random.uniform(jax.random.fold_in(own, axis_at), (blocks,), jnp.float32, low / len(cuts), largest / len(cuts)))
        gain = gain * jnp.repeat(draws, dims[axis_at] // blocks).reshape([-1 if axis == axis_at else 1 for axis in range(len(dims))])
    return gain


def noise(key, dims, scale, reach, pieces=(), kind=jnp.bfloat16):
    drawn = scale * jax.random.normal(key, dims, jnp.float32)
    if pieces:
        drawn = drawn * steps_of(key, dims, pieces, -0.22, 0.18)
    return jnp.clip(drawn, -reach, reach).astype(kind)


def setup_inputs(seed: int = 0) -> dict:
    splits = jax.random.split(jax.random.key(seed), 12)
    coarse_vertex_embedding = noise(splits[0], (REALISATION_TOTAL, NODES, C), 1.0, 6.0, ((0, 8), (1, 96)))
    lattice_bypass_embedding = noise(splits[1], (REALISATION_TOTAL, GRID, C), 1.0, 6.0, ((0, 8), (1, 96)))
    initial_condition = noise(splits[2], (REALISATION_TOTAL, GRID, V), 1.0, 6.0, ((0, 8), (1, 96)), jnp.float32)
    verifying_analysis = noise(splits[3], (GRID, V), 1.5, 8.0, ((0, 96),), jnp.float32)
    edge_index = set_ends(jax.random.randint(splits[4], (GRID, EDGES), 0, 3 * MESH_DEV), jax.random.fold_in(splits[4], 1), 0, (3 * MESH_DEV) - 1).astype(jnp.int32)
    area_weight = jnp.clip(jnp.exp(math.log(4.0) - 2.3025851 * jax.random.uniform(splits[5], (GRID,), jnp.float32) ** steps_of(splits[5], (GRID,), ((0, 96),), -0.2, 0.2)), 0.4, 4.0)
    variable_weight = jnp.clip(jnp.exp(jax.random.uniform(splits[6], (V,), jnp.float32, math.log(0.2), math.log(2.0))), 0.2, 2.0)
    query_weight = noise(splits[7], (C, C), (max(C // 100, 1)) ** -0.5, 2.0)
    keyval_weight = noise(splits[8], (C, 2 * C), C ** -0.5, 0.1875)
    output_weight = noise(splits[9], (C, C), C ** -0.5, 0.1875)
    output_channel_matrix = noise(splits[10], (C, V), C ** -0.5, 0.1875)
    return dict(coarse_vertex_embedding=coarse_vertex_embedding, lattice_bypass_embedding=lattice_bypass_embedding, initial_condition=initial_condition, verifying_analysis=verifying_analysis, edge_index=edge_index, area_weight=area_weight, variable_weight=variable_weight, query_weight=query_weight, keyval_weight=keyval_weight, output_weight=output_weight, output_channel_matrix=output_channel_matrix)


SOFT_CAP = 30.0
SOFTENED_QUAD = 0.01
FAIR_ALPHA = 0.95
OBJECTIVE_WEIGHT = 64.0
EXACT_PRODUCT = lax.Precision.HIGHEST

def attend(query, keys, values):
    number, edge_count, channels = keys.shape
    head_size = channels // HEADS
    query_heads = query.reshape(number, HEADS, head_size)
    key_heads = keys.astype(jnp.float32).reshape(number, edge_count, HEADS, head_size)
    value_heads = values.astype(jnp.float32).reshape(number, edge_count, HEADS, head_size)
    score = jnp.einsum('ghd,gehd->geh', query_heads, key_heads, precision=EXACT_PRODUCT) / math.sqrt(head_size)
    capped = SOFT_CAP * jnp.tanh(score / SOFT_CAP)
    exponent = jnp.exp(capped)
    weight = exponent / lax.optimization_barrier(jnp.sum(exponent, axis=1, keepdims=True))
    mixture = jnp.einsum('geh,gehd->ghd', weight, value_heads, precision=EXACT_PRODUCT).reshape(number, channels)
    return (mixture, (query_heads, key_heads, value_heads, weight, capped))

def attend_back(grad_mixture, retained_activations):
    query_heads, key_heads, value_heads, weight, capped = retained_activations
    number, edge_count, head_count, head_size = key_heads.shape
    grad_heads = grad_mixture.reshape(number, head_count, head_size)
    grad_weight = jnp.einsum('ghd,gehd->geh', grad_heads, value_heads, precision=EXACT_PRODUCT)
    grad_values = jnp.einsum('geh,ghd->gehd', weight, grad_heads, precision=EXACT_PRODUCT)
    grad_capped = weight * (grad_weight - lax.optimization_barrier(jnp.sum(weight * grad_weight, axis=1, keepdims=True)))
    grad_score = grad_capped * (1.0 - (capped / SOFT_CAP) ** 2) / math.sqrt(head_size)
    grad_query = jnp.einsum('geh,gehd->ghd', grad_score, key_heads, precision=EXACT_PRODUCT)
    grad_keys = jnp.einsum('geh,ghd->gehd', grad_score, query_heads, precision=EXACT_PRODUCT)
    shape_out = (number, edge_count, head_count * head_size)
    return (grad_query.reshape(number, head_count * head_size), grad_keys.reshape(shape_out), grad_values.reshape(shape_out))

def unpack_onward(picked, lattice_site_lines, condition_line_tile, query_weight, output_weight, output_channel_matrix):
    channels = lattice_site_lines.shape[1]
    keys = picked[:, :, :channels]
    values = picked[:, :, channels:]
    query = jnp.dot(lattice_site_lines, query_weight, preferred_element_type=jnp.float32)
    mixture, retained_activations = attend(query, keys, values)
    internal_embedding = (lattice_site_lines.astype(jnp.float32) + jnp.dot(mixture.astype(jnp.bfloat16), output_weight, preferred_element_type=jnp.float32)).astype(jnp.bfloat16)
    realisation_prediction = condition_line_tile + jnp.dot(internal_embedding, output_channel_matrix, preferred_element_type=jnp.float32)
    return (realisation_prediction, retained_activations)

def decode_back(slope, retained_activations, query_weight, output_weight, output_channel_matrix):
    grad_hidden = jnp.dot(slope, output_channel_matrix.T, preferred_element_type=jnp.float32)
    grad_mixture = jnp.dot(grad_hidden.astype(jnp.bfloat16), output_weight.T, preferred_element_type=jnp.float32)
    grad_query, grad_keys, grad_values = attend_back(grad_mixture, retained_activations)
    grad_rows = (grad_hidden + jnp.dot(grad_query.astype(jnp.bfloat16), query_weight.T, preferred_element_type=jnp.float32)).astype(jnp.bfloat16)
    grad_pairs = jnp.concatenate([grad_keys, grad_values], axis=2)
    return (grad_rows, grad_pairs.reshape(-1, grad_pairs.shape[2]))

def penalty_surface(piled_realisations, analysis_lines):
    realisation_tally = piled_realisations.shape[0]
    fair_eps = (1.0 - FAIR_ALPHA) / realisation_tally
    accuracy_term = lax.optimization_barrier(jnp.mean(jnp.sqrt((piled_realisations - analysis_lines[None]) ** 2 + SOFTENED_QUAD), axis=0))
    spread = jnp.zeros_like(analysis_lines)
    for index_a in range(realisation_tally):
        for index_b in range(index_a + 1, realisation_tally):
            spread = spread + jnp.sqrt((piled_realisations[index_a] - piled_realisations[index_b]) ** 2 + SOFTENED_QUAD)
    return accuracy_term - (1.0 - fair_eps) / (realisation_tally * (realisation_tally - 1)) * spread

def penalty_derivative(realisation_prediction, piled_realisations, analysis_lines):
    realisation_tally = piled_realisations.shape[0]
    fair_eps = (1.0 - FAIR_ALPHA) / realisation_tally
    prediction_misfit = realisation_prediction - analysis_lines
    accuracy_term = prediction_misfit / jnp.sqrt(prediction_misfit * prediction_misfit + SOFTENED_QUAD) / realisation_tally
    realisation_dispersion = realisation_prediction[None] - piled_realisations
    spread = lax.optimization_barrier(jnp.sum(realisation_dispersion / jnp.sqrt(realisation_dispersion * realisation_dispersion + SOFTENED_QUAD), axis=0))
    return accuracy_term - (1.0 - fair_eps) / (realisation_tally * (realisation_tally - 1)) * spread

def reference(coarse_vertex_embedding, lattice_bypass_embedding, initial_condition, verifying_analysis, edge_index, area_weight, variable_weight, query_weight, keyval_weight, output_weight, output_channel_matrix):
    sector = (jnp.arange(GRID, dtype=jnp.int32) // GRID_DEV)[:, None]
    source = ((sector * MESH_DEV + edge_index - MESH_DEV) % NODES).astype(jnp.int32)

    def advance_realisation(coarse_vertex_lines, lattice_site_lines, condition_line_tile):
        keyval = jnp.dot(coarse_vertex_lines, keyval_weight, preferred_element_type=jnp.float32).astype(jnp.bfloat16)
        picked = jnp.take(keyval, source.reshape(-1), axis=0).reshape(GRID, EDGES, 2 * C)
        return unpack_onward(picked, lattice_site_lines, condition_line_tile, query_weight, output_weight, output_channel_matrix)
    prediction_pile = lax.map(lambda realisation_entry: advance_realisation(realisation_entry[0], realisation_entry[1], realisation_entry[2])[0], (coarse_vertex_embedding, lattice_bypass_embedding, initial_condition))
    multiplier_value = area_weight[:, None] * variable_weight[None, :]
    probabilistic_penalty = multiplier_value * penalty_surface(prediction_pile, verifying_analysis)
    derivative_pile = jnp.stack([(OBJECTIVE_WEIGHT * multiplier_value * penalty_derivative(prediction_pile[realisation_ordinal], prediction_pile, verifying_analysis)).astype(jnp.bfloat16) for realisation_ordinal in range(REALISATION_TOTAL)])

    def member_back(realisation_entry):
        coarse_vertex_lines, lattice_site_lines, condition_line_tile, slope = realisation_entry
        realisation_prediction, retained_activations = advance_realisation(coarse_vertex_lines, lattice_site_lines, condition_line_tile)
        grad_rows, grad_pairs = decode_back(slope, retained_activations, query_weight, output_weight, output_channel_matrix)
        blocks = (grad_pairs.reshape(N_SPACE, GRID_DEV * EDGES, 2 * C), edge_index.reshape(N_SPACE, GRID_DEV * EDGES))

        def block_term(block):
            partial_value = jax.ops.segment_sum(block[0], block[1], num_segments=3 * MESH_DEV).astype(jnp.bfloat16)
            return jnp.dot(partial_value, keyval_weight.T, preferred_element_type=jnp.float32).astype(jnp.bfloat16)
        rounded = lax.optimization_barrier(lax.map(block_term, blocks))
        terms = rounded.astype(jnp.float32).reshape(N_SPACE, 3, MESH_DEV, C)
        total = terms[:, 1] + jnp.roll(terms[:, 0], -1, axis=0) + jnp.roll(terms[:, 2], 1, axis=0)
        return (total.reshape(NODES, C).astype(jnp.bfloat16), grad_rows)
    grad_mesh, grad_grid = lax.map(member_back, (coarse_vertex_embedding, lattice_bypass_embedding, initial_condition, derivative_pile))
    return (grad_mesh, grad_grid, probabilistic_penalty)
```

```python
import jax
import jax.numpy as jnp
from jax import lax
from jax.experimental import pallas as pl
from jax.experimental.pallas import tpu as pltpu
from jax.sharding import PartitionSpec as P

HEADS = 16
PAIRS = HEADS // 2
SOFT_CAP = 30.0
SOFTENED_QUAD = 0.01
FAIR_ALPHA = 0.95
OBJECTIVE_WEIGHT = 64.0
ROWS = 112

F32 = jnp.float32
BF16 = jnp.bfloat16
MIB = 1024 * 1024

NN = (((1,), (0,)), ((), ()))
NT = (((1,), (1,)), ((), ()))
TN = (((0,), (0,)), ((), ()))


def mm(a, b, dims=NN):
    return lax.dot_general(a, b, dims, preferred_element_type=F32)


def split(x):
    hi = x.astype(BF16)
    return hi, (x - hi.astype(F32)).astype(BF16)


def diagonal(top, bottom):
    zero = jnp.zeros_like(top)
    return jnp.concatenate(
        [jnp.concatenate([top, zero], 1), jnp.concatenate([zero, bottom], 1)], 0
    )


def quadrants(full):
    return jnp.concatenate([full[:64, :128], full[64:, 128:]], 0)


def lane_halves(block, keep):
    return jnp.concatenate([block * keep, block * (1 - keep)], 0)


def prepare_kernel(
    lattice, query_weight, output_weight, channels_t, condition_t, area, variable,
    query, query_hi, query_lo, joint_t, joint, base_t, scale_t, wide,
):
    rows = lattice[...]
    q = mm(rows, query_weight[...])
    query[...] = q.astype(BF16)
    hi, lo = split(q.T)
    query_hi[...] = hi
    query_lo[...] = lo
    variables = channels_t.shape[0]
    base_t[...] = jnp.zeros_like(base_t)
    base_t[:variables] = condition_t[...] + mm(channels_t[...], rows, NT)
    wide[...] = jnp.zeros_like(wide)
    wide[:variables] = mm(channels_t[...], output_weight[...], NT)
    both = wide[...]
    hi, lo = split(both)
    joint_t[:ROWS] = hi[:ROWS]
    joint_t[ROWS:] = lo[:ROWS]
    hi, lo = split(both.T)
    joint[:, :128] = hi
    joint[:, 128:] = lo
    wide[:, :128] = jnp.zeros((128, 128), F32)
    wide[:, :variables] = jnp.broadcast_to(variable[...], (128, variables))
    scale_t[...] = (wide[:, :128].T * area[...])[:ROWS]


def forward_kernel(
    before, own, after, keyval_weight, query_hi, query_lo, joint_t, base_t, edges_t,
    piled, mine, keyval, weight, slant,
    nodes, mixture_t,
):
    block = own.shape[0]
    nodes[:block] = before[...]
    nodes[block : 2 * block] = own[...]
    nodes[2 * block :] = after[...]
    slots = nodes.shape[0]
    channels = nodes.shape[1]
    points = edges_t.shape[1]
    number = lax.broadcasted_iota(jnp.int32, (slots, points), 0)
    count = jnp.zeros((slots, points), F32)
    for e in range(edges_t.shape[0]):
        count = count + (number == edges_t[e : e + 1, :]).astype(F32)
    count = jnp.concatenate([count, count], 1)
    x = nodes[...]
    for p in range(PAIRS):
        at = slice(128 * p, 128 * p + 128)
        v_at = slice(channels + 128 * p, channels + 128 * p + 128)
        k = mm(x, keyval_weight[:, at]).astype(BF16)
        v = mm(x, keyval_weight[:, v_at]).astype(BF16)
        keyval[:, at] = k
        keyval[:, v_at] = v
        q_hi = query_hi[at, :]
        q_lo = query_lo[at, :]
        score = mm(
            jnp.concatenate([k, k], 1),
            jnp.concatenate([diagonal(q_hi[:64], q_hi[64:]), diagonal(q_lo[:64], q_lo[64:])], 0),
        )
        bent = jnp.tanh(score * (1.0 / (8.0 * SOFT_CAP)))
        exponent = jnp.exp(SOFT_CAP * bent) * count
        w = exponent / jnp.sum(exponent, axis=0, keepdims=True)
        weight[p] = w
        slant[p] = w * ((1.0 - bent * bent) * 0.125)
        mixture_t[at, :] = quadrants(mm(v, w.astype(BF16), TN)).astype(BF16)
    parts = mm(joint_t[...], mixture_t[...])
    forecast = (base_t[...] + (parts[:ROWS] + parts[ROWS:])).astype(BF16)
    mine[...] = forecast
    for m in range(piled.shape[0]):
        piled[m] = forecast


def backward_kernel(
    piled, mine, analysis_t, scale_t, joint, joint_t, query, keyval, weight, slant, keyval_weight,
    term_before, term_own, term_after, grad_query_t, slope,
    partial, slope_t, truth,
):
    members = piled.shape[0]
    fair_eps = (1.0 - FAIR_ALPHA) / members
    variables = analysis_t.shape[0]
    truth[...] = jnp.zeros_like(truth)
    truth[:variables] = analysis_t[...]
    forecast = mine[...].astype(F32)

    def bend(d):
        return d * lax.rsqrt(d * d + SOFTENED_QUAD)

    spread = jnp.zeros_like(forecast)
    for k in range(members):
        spread = spread + bend(forecast - piled[k].astype(F32))
    out = bend(forecast - truth[...]) * (1.0 / members) - (
        (1.0 - fair_eps) / (members * (members - 1))
    ) * spread
    slope_t[...] = jnp.zeros_like(slope_t)
    slope_t[:ROWS] = (OBJECTIVE_WEIGHT * scale_t[...]) * out
    s_t = slope_t[...]
    s = s_t.T.astype(BF16)
    s_t = s_t.astype(BF16)
    slope[...] = s
    channels = query.shape[1]
    keep = (lax.broadcasted_iota(jnp.int32, (128, 128), 1) < 64).astype(F32).astype(BF16)
    s_both = jnp.concatenate([s_t, s_t], 0)
    for p in range(PAIRS):
        at = slice(128 * p, 128 * p + 128)
        v_at = slice(channels + 128 * p, channels + 128 * p + 128)
        gm_t = mm(joint[at, :], s_both).astype(BF16)
        gm = mm(s[:, :ROWS], joint_t[:ROWS, at]).astype(BF16)
        k = keyval[:, at]
        v = keyval[:, v_at]
        w = weight[p]
        gw = mm(v, diagonal(gm_t[:64], gm_t[64:]))
        gs = (slant[p] * (gw - jnp.sum(w * gw, axis=0, keepdims=True))).astype(BF16)
        grad_query_t[at, :] = quadrants(mm(k, gs, TN)).astype(BF16)
        partial[:, at] = mm(gs, lane_halves(query[:, at], keep)).astype(BF16)
        partial[:, v_at] = mm(w.astype(BF16), lane_halves(gm, keep)).astype(BF16)
    terms = mm(partial[...], keyval_weight[...], NT).astype(BF16)
    block = term_own.shape[0]
    term_before[...] = terms[:block]
    term_own[...] = terms[block : 2 * block]
    term_after[...] = terms[2 * block :]


def finish_kernel(
    member, grad_query_t, query_weight, slope, channels_t, piled, analysis_t, scale_t,
    grad_grid, penalty,
    truth, turned,
):
    variables = analysis_t.shape[0]
    rows_t = mm(query_weight[...], grad_query_t[...])
    hidden = mm(slope[:, :variables], channels_t[...])
    grad_grid[...] = (rows_t.T + hidden).astype(BF16)
    members = piled.shape[0]
    fair_eps = (1.0 - FAIR_ALPHA) / members
    truth[...] = jnp.zeros_like(truth)
    truth[:variables] = analysis_t[...]

    def soft(d):
        return jnp.sqrt(d * d + SOFTENED_QUAD)

    casts = [piled[m].astype(F32) for m in range(members)]
    goal = truth[...]
    accuracy = jnp.zeros_like(goal)
    spread = jnp.zeros_like(goal)
    for a in range(members):
        accuracy = accuracy + soft(casts[a] - goal)
        for b in range(a + 1, members):
            spread = spread + soft(casts[a] - casts[b])
    turned[...] = jnp.zeros_like(turned)
    turned[:ROWS] = scale_t[...] * (
        accuracy * (1.0 / members) - ((1.0 - fair_eps) / (members * (members - 1))) * spread
    )
    turned[...] = turned[...].T
    rows = penalty.shape[0]
    start = pl.multiple_of(member[0] * rows, rows)
    penalty[...] = turned[pl.ds(start, rows), :variables]


def shaped(*dims, dtype=BF16):
    return jax.ShapeDtypeStruct(dims, dtype)


def call(kernel, outs, scratch, args, limit, flops, moved, specs=None):
    return pl.pallas_call(
        kernel,
        out_shape=outs,
        in_specs=specs or [pl.BlockSpec(memory_space=pltpu.VMEM)] * len(args),
        out_specs=[pl.BlockSpec(memory_space=pltpu.VMEM)] * len(outs),
        scratch_shapes=scratch,
        compiler_params=pltpu.CompilerParams(vmem_limit_bytes=limit * MIB),
        cost_estimate=pl.CostEstimate(flops=flops, bytes_accessed=moved, transcendentals=0),
    )(*args)


def shift(value, axis, by):
    count = lax.axis_size(axis)
    return lax.ppermute(value, axis, [(i, (i + by) % count) for i in range(count)])


def per_device(
    coarse_vertex_embedding,
    lattice_bypass_embedding,
    initial_condition,
    verifying_analysis,
    edge_index,
    area_weight,
    variable_weight,
    query_weight,
    keyval_weight,
    output_weight,
    output_channel_matrix,
):
    own = coarse_vertex_embedding[0]
    lattice = lattice_bypass_embedding[0]
    block, channels = own.shape
    points = lattice.shape[0]
    slots = 3 * block
    members = lax.axis_size("member")
    condition_t = initial_condition[0].T
    analysis_t = verifying_analysis.T
    edges_t = edge_index.T
    channels_t = output_channel_matrix.T

    before = shift(own, "space", 1)
    after = shift(own, "space", -1)

    query, query_hi, query_lo, joint_t, joint, base_t, scale_t = call(
        prepare_kernel,
        [
            shaped(points, channels),
            shaped(channels, points),
            shaped(channels, points),
            shaped(2 * ROWS, channels),
            shaped(channels, 256),
            shaped(ROWS, points, dtype=F32),
            shaped(ROWS, points, dtype=F32),
        ],
        [pltpu.VMEM((128, channels), F32)],
        (
            lattice,
            query_weight,
            output_weight,
            channels_t,
            condition_t,
            area_weight[None],
            variable_weight[None],
        ),
        24,
        600_000_000,
        6_000_000,
    )
    piled, mine, keyval, weight, slant = call(
        forward_kernel,
        [
            shaped(members, ROWS, points),
            shaped(ROWS, points),
            shaped(slots, 2 * channels),
            shaped(PAIRS, slots, 2 * points, dtype=F32),
            shaped(PAIRS, slots, 2 * points, dtype=F32),
        ],
        [pltpu.VMEM((slots, channels), BF16), pltpu.VMEM((channels, points), BF16)],
        (before, own, after, keyval_weight, query_hi, query_lo, joint_t, base_t, edges_t),
        24,
        1_000_000_000,
        8_000_000,
    )
    piled = lax.all_to_all(piled, "member", split_axis=0, concat_axis=0, tiled=True)
    term_before, term_own, term_after, grad_query_t, slope = call(
        backward_kernel,
        [
            shaped(block, channels),
            shaped(block, channels),
            shaped(block, channels),
            shaped(channels, points),
            shaped(points, 128),
        ],
        [
            pltpu.VMEM((slots, 2 * channels), BF16),
            pltpu.VMEM((128, points), F32),
            pltpu.VMEM((ROWS, points), F32),
        ],
        (
            piled, mine, analysis_t, scale_t, joint, joint_t, query, keyval, weight, slant,
            keyval_weight,
        ),
        24,
        1_500_000_000,
        8_000_000,
    )
    from_next = shift(term_before, "space", -1)
    from_prev = shift(term_after, "space", 1)
    member = lax.axis_index("member").astype(jnp.int32).reshape(1)
    vmem = pl.BlockSpec(memory_space=pltpu.VMEM)
    grad_grid, penalty = call(
        finish_kernel,
        [shaped(points, channels), shaped(points // members, variable_weight.shape[0], dtype=F32)],
        [pltpu.VMEM((ROWS, points), F32), pltpu.VMEM((128, 128), F32)],
        (member, grad_query_t, query_weight, slope, channels_t, piled, analysis_t, scale_t),
        24,
        400_000_000,
        4_000_000,
        specs=[pl.BlockSpec(memory_space=pltpu.SMEM)] + [vmem] * 7,
    )
    grad_nodes = term_own.astype(F32) + from_next.astype(F32) + from_prev.astype(F32)
    return (grad_nodes.astype(BF16)[None], grad_grid[None], penalty)


def solution(mesh):
    return jax.shard_map(
        per_device,
        mesh=mesh,
        in_specs=(
            P("member", "space", None),
            P("member", "space", None),
            P("member", "space", None),
            P("space", None),
            P("space", None),
            P("space"),
            P(),
            P(),
            P(),
            P(),
            P(),
        ),
        out_specs=(
            P("member", "space", None),
            P("member", "space", None),
            P(("space", "member"), None),
        ),
        check_vma=False,
    )
```

```python
import jax
import jax.numpy as jnp
from jax import lax
from jax.experimental import pallas as pl
from jax.experimental.pallas import tpu as pltpu
from jax.sharding import PartitionSpec as P

HEADS = 16
PAIRS = HEADS // 2
SOFT_CAP = 30.0
SOFTENED_QUAD = 0.01
FAIR_ALPHA = 0.95
OBJECTIVE_WEIGHT = 64.0
ROWS = 112
CHUNK = 512

F32 = jnp.float32
BF16 = jnp.bfloat16
MIB = 1024 * 1024

NN = (((1,), (0,)), ((), ()))
NT = (((1,), (1,)), ((), ()))
TN = (((0,), (0,)), ((), ()))


def mm(a, b, dims=NN):
    return lax.dot_general(a, b, dims, preferred_element_type=F32)


def split(x):
    hi = x.astype(BF16)
    return hi, (x - hi.astype(F32)).astype(BF16)


def diagonal(top, bottom):
    zero = jnp.zeros_like(top)
    return jnp.concatenate(
        [jnp.concatenate([top, zero], 1), jnp.concatenate([zero, bottom], 1)], 0
    )


def quadrants(full):
    return jnp.concatenate([full[:64, :128], full[64:, 128:]], 0)


def lanes_kernel(keep):
    first = (lax.broadcasted_iota(jnp.int32, (128, 128), 1) < 64).astype(F32)
    keep[:128] = first.astype(BF16)
    keep[128:] = (1.0 - first).astype(BF16)


def prepare_kernel(
    lattice, query_weight, channels_t, condition_t, query, query_hi, query_lo, base_t
):
    rows = lattice[...]
    for c in range(query_weight.shape[1] // CHUNK):
        at = slice(CHUNK * c, CHUNK * c + CHUNK)
        q = mm(rows, query_weight[:, at])
        query[:, at] = q.astype(BF16)
        hi, lo = split(q.T)
        query_hi[at, :] = hi
        query_lo[at, :] = lo
    variables = channels_t.shape[0]
    base_t[...] = jnp.zeros_like(base_t)
    base_t[:variables] = condition_t[:, 0, :] + mm(channels_t[...], rows, NT)


def attend_kernel(
    info, across, beside, own, keyval_weight, query, query_hi, query_lo, edges_t, keep, area,
    variable,
    keyval, weight, weight_16, slant, mixture_t, query_halves, scale_t,
    nodes, score,
):
    block = own.shape[0]
    odd = info[1]
    nodes[block : 2 * block] = own[...]
    nodes[pl.ds(pl.multiple_of(odd * 2 * block, block), block)] = across[...]
    nodes[pl.ds(pl.multiple_of((1 - odd) * 2 * block, block), block)] = beside[...]
    slots, channels = nodes.shape
    points = edges_t.shape[1]
    x = nodes[...]
    for c in range(2 * channels // CHUNK):
        at = slice(CHUNK * c, CHUNK * c + CHUNK)
        keyval[:, at] = mm(x, keyval_weight[:, at]).astype(BF16)
    for p in range(PAIRS):
        at = slice(128 * p, 128 * p + 128)
        k = keyval[:, at]
        q_hi = query_hi[at, :]
        q_lo = query_lo[at, :]
        score[p] = mm(
            jnp.concatenate([k, k], 1),
            jnp.concatenate([diagonal(q_hi[:64], q_hi[64:]), diagonal(q_lo[:64], q_lo[64:])], 0),
        )
    number = lax.broadcasted_iota(jnp.int32, (slots, points), 0)
    count = jnp.zeros((slots, points), F32)
    for e in range(edges_t.shape[0]):
        count = count + (number == edges_t[e : e + 1, :]).astype(F32)
    count = jnp.concatenate([count, count], 1)
    for p in range(PAIRS):
        bent = jnp.tanh(score[p] * (1.0 / (8.0 * SOFT_CAP)))
        exponent = jnp.exp(SOFT_CAP * bent) * count
        w = exponent * (1.0 / jnp.sum(exponent, axis=0, keepdims=True))
        weight[p] = w
        weight_16[p] = w.astype(BF16)
        slant[p] = w * ((1.0 - bent * bent) * 0.125)
    left = keep[:128]
    right = keep[128:]
    for p in range(PAIRS):
        at = slice(128 * p, 128 * p + 128)
        v = keyval[:, channels + 128 * p : channels + 128 * p + 128]
        mixture_t[at, :] = quadrants(mm(v, weight_16[p], TN)).astype(BF16)
        query_halves[p] = jnp.concatenate([query[:, at] * left, query[:, at] * right], 0)
    variables = variable.shape[1]
    spread = jnp.concatenate(
        [
            jnp.broadcast_to(variable[...], (128, variables)),
            jnp.zeros((128, 128 - variables), F32),
        ],
        1,
    )
    scale_t[...] = spread.T[:ROWS] * area[...]


def joint_kernel(output_weight, channels_t, joint_t):
    variables, channels = channels_t.shape
    both = mm(channels_t[...], output_weight[...], NT)
    hi, lo = split(jnp.concatenate([both, jnp.zeros((ROWS - variables, channels), F32)], 0))
    joint_t[:ROWS] = hi
    joint_t[ROWS:] = lo


def forecast_kernel(joint_t, base_t, mixture_t, keyval, keep, piled, mine, value_joint):
    channels = mixture_t.shape[0]
    parts = mm(joint_t[...], mixture_t[...])
    forecast = (base_t[...] + (parts[:ROWS] + parts[ROWS:])).astype(BF16)
    mine[...] = forecast
    for m in range(piled.shape[0]):
        piled[m] = forecast
    slots = keyval.shape[0]
    pad = jnp.zeros((slots, 128 - ROWS), BF16)
    for p in range(PAIRS):
        at = slice(128 * p, 128 * p + 128)
        v = keyval[:, channels + 128 * p : channels + 128 * p + 128]
        hi = joint_t[:ROWS, at]
        lo = joint_t[ROWS:, at]
        for half in range(2):
            side = keep[128 * half : 128 * half + ROWS]
            high, low = split(
                mm(
                    jnp.concatenate([v, v], 1),
                    jnp.concatenate([hi * side, lo * side], 1),
                    NT,
                )
            )
            rows = slice((2 * p + half) * slots, (2 * p + half + 1) * slots)
            value_joint[rows, :] = jnp.concatenate([high, pad, low, pad], 1)


def backward_kernel(
    info, piled, mine, analysis_t, scale_t, joint_t, query_halves, value_joint, weight, weight_16,
    slant, keyval_weight, keep,
    term_across, term_beside, term_own, grad_score, slope,
    partial, slope_t, truth, terms, grad_weight,
):
    members = piled.shape[0]
    fair_eps = (1.0 - FAIR_ALPHA) / members
    variables = analysis_t.shape[0]
    truth[...] = jnp.zeros_like(truth)
    truth[:variables] = analysis_t[...]

    def bend(d):
        return d * lax.rsqrt(d * d + SOFTENED_QUAD)

    slope_t[ROWS:] = jnp.zeros((128 - ROWS, slope_t.shape[1]), F32)
    for r in range(0, ROWS, 16):
        at = slice(r, r + 16)
        forecast = mine[at].astype(F32)
        spread = jnp.zeros_like(forecast)
        for k in range(members):
            spread = spread + bend(forecast - piled[k, at].astype(F32))
        slope_t[at] = (OBJECTIVE_WEIGHT * scale_t[at]) * (
            bend(forecast - truth[at]) * (1.0 / members)
            - ((1.0 - fair_eps) / (members * (members - 1))) * spread
        )
    s_t = slope_t[...]
    s = s_t.T.astype(BF16)
    s_t = s_t.astype(BF16)
    slope[...] = s
    channels = keyval_weight.shape[1] // 2
    slots = partial.shape[0]
    grad_weight[...] = mm(value_joint[...], jnp.concatenate([s_t, s_t], 0))
    left = keep[:128]
    right = keep[128:]
    gm = mm(s[:, :ROWS], joint_t[:ROWS]).astype(BF16)
    for p in range(PAIRS):
        at = slice(128 * p, 128 * p + 128)
        v_at = slice(channels + 128 * p, channels + 128 * p + 128)
        halves = jnp.concatenate([gm[:, at] * left, gm[:, at] * right], 0)
        partial[:, v_at] = mm(weight_16[p], halves).astype(BF16)
    for p in range(PAIRS):
        low = 2 * p * slots
        gw = jnp.concatenate(
            [grad_weight[low : low + slots], grad_weight[low + slots : low + 2 * slots]], 1
        )
        w = weight[p]
        grad_score[p] = (
            slant[p] * (gw - jnp.sum(w * gw, axis=0, keepdims=True))
        ).astype(BF16)
    for p in range(PAIRS):
        at = slice(128 * p, 128 * p + 128)
        partial[:, at] = mm(grad_score[p], query_halves[p]).astype(BF16)
    terms[...] = (
        mm(partial[:, channels:], keyval_weight[:, channels:], NT)
        + mm(partial[:, :channels], keyval_weight[:, :channels], NT)
    ).astype(BF16)
    block = term_own.shape[0]
    odd = info[1]
    term_own[...] = terms[block : 2 * block]
    term_across[...] = terms[pl.ds(pl.multiple_of(odd * 2 * block, block), block)]
    term_beside[...] = terms[pl.ds(pl.multiple_of((1 - odd) * 2 * block, block), block)]


def finish_kernel(
    info, keyval, grad_score, query_weight, slope, channels_t, piled, analysis_t, scale_t,
    grad_grid, penalty,
    grad_query, truth, turned,
):
    variables = channels_t.shape[0]
    for p in range(PAIRS):
        at = slice(128 * p, 128 * p + 128)
        grad_query[:, at] = quadrants(mm(keyval[:, at], grad_score[p], TN)).T.astype(BF16)
    hidden = mm(slope[:, :variables], channels_t[...])
    for c in range(query_weight.shape[0] // CHUNK):
        at = slice(CHUNK * c, CHUNK * c + CHUNK)
        grad_grid[:, at] = (
            mm(grad_query[...], query_weight[at, :], NT) + hidden[:, at]
        ).astype(BF16)
    members = piled.shape[0]
    fair_eps = (1.0 - FAIR_ALPHA) / members
    truth[...] = jnp.zeros_like(truth)
    truth[:variables] = analysis_t[...]

    def soft(d):
        square = d * d + SOFTENED_QUAD
        return square * lax.rsqrt(square)

    turned[ROWS:] = jnp.zeros((128 - ROWS, 128), F32)
    for r in range(0, ROWS, 16):
        at = slice(r, r + 16)
        casts = [piled[m, at].astype(F32) for m in range(members)]
        goal = truth[at]
        accuracy = jnp.zeros_like(goal)
        spread = jnp.zeros_like(goal)
        for a in range(members):
            accuracy = accuracy + soft(casts[a] - goal)
            for b in range(a + 1, members):
                spread = spread + soft(casts[a] - casts[b])
        turned[at] = scale_t[at] * (
            accuracy * (1.0 / members) - ((1.0 - fair_eps) / (members * (members - 1))) * spread
        )
    turned[...] = turned[...].T
    rows = penalty.shape[0]
    start = pl.multiple_of(info[0] * rows, rows)
    penalty[...] = turned[pl.ds(start, rows), :variables]


def shaped(*dims, dtype=BF16):
    return jax.ShapeDtypeStruct(dims, dtype)


VMEM = pl.BlockSpec(memory_space=pltpu.VMEM)
HBM = pl.BlockSpec(memory_space=pltpu.HBM)
SMEM = pl.BlockSpec(memory_space=pltpu.SMEM)


def call(kernel, outs, scratch, args, limit, flops, moved, specs):
    specs = list(specs) + [VMEM] * (len(args) - len(specs))
    return pl.pallas_call(
        kernel,
        out_shape=outs,
        in_specs=specs,
        out_specs=[VMEM] * len(outs),
        scratch_shapes=scratch,
        compiler_params=pltpu.CompilerParams(vmem_limit_bytes=limit * MIB),
        cost_estimate=pl.CostEstimate(flops=flops, bytes_accessed=moved, transcendentals=0),
    )(*args)


def swap_across(value):
    count = lax.axis_size("space")
    return lax.ppermute(
        value, "space", [(i, (i + 1) % count if i % 2 else (i - 1) % count) for i in range(count)]
    )


def swap_beside(value):
    return lax.ppermute(value, "space", [(i, i ^ 1) for i in range(lax.axis_size("space"))])


def per_device(
    coarse_vertex_embedding,
    lattice_bypass_embedding,
    initial_condition,
    verifying_analysis,
    edge_index,
    area_weight,
    variable_weight,
    query_weight,
    keyval_weight,
    output_weight,
    output_channel_matrix,
):
    own = coarse_vertex_embedding[0]
    lattice = lattice_bypass_embedding[0]
    block, channels = own.shape
    points = lattice.shape[0]
    variables = variable_weight.shape[0]
    slots = 3 * block
    members = lax.axis_size("member")
    condition_t = jnp.transpose(initial_condition, (2, 0, 1))
    analysis_t = verifying_analysis.T
    edges_t = edge_index.T
    channels_t = output_channel_matrix.T
    info = jnp.stack([lax.axis_index("member"), lax.axis_index("space") % 2]).astype(jnp.int32)

    across = swap_across(own)
    (keep,) = call(lanes_kernel, [shaped(256, 128)], [], (), 1, 3_000_000_000, 12_000_000, [])
    own, keep = lax.optimization_barrier((own, keep))
    beside = swap_beside(own)
    query, query_hi, query_lo, base_t = call(
        prepare_kernel,
        [
            shaped(points, channels),
            shaped(channels, points),
            shaped(channels, points),
            shaped(ROWS, points, dtype=F32),
        ],
        [],
        (lattice, query_weight, channels_t, condition_t),
        4,
        1_000_000,
        1_000_000,
        [],
    )
    (joint_t,) = call(
        joint_kernel,
        [shaped(2 * ROWS, channels)],
        [],
        (output_weight, channels_t),
        4,
        3_000_000_000,
        10_000_000,
        [],
    )
    keyval, weight, weight_16, slant, mixture_t, query_halves, scale_t = call(
        attend_kernel,
        [
            shaped(slots, 2 * channels),
            shaped(PAIRS, slots, 2 * points, dtype=F32),
            shaped(PAIRS, slots, 2 * points),
            shaped(PAIRS, slots, 2 * points, dtype=F32),
            shaped(channels, points),
            shaped(PAIRS, 256, 128),
            shaped(ROWS, points, dtype=F32),
        ],
        [
            pltpu.VMEM((slots, channels), BF16),
            pltpu.VMEM((PAIRS, slots, 2 * points), F32),
        ],
        (
            info, across, beside, own, keyval_weight, query, query_hi, query_lo, edges_t, keep,
            area_weight[None], variable_weight[None],
        ),
        4,
        2_000_000_000,
        8_000_000,
        [SMEM],
    )
    piled, mine, value_joint = call(
        forecast_kernel,
        [
            shaped(members, ROWS, points),
            shaped(ROWS, points),
            shaped(HEADS * slots, 256),
        ],
        [],
        (joint_t, base_t, mixture_t, keyval, keep),
        4,
        500_000_000,
        4_000_000,
        [],
    )
    piled = lax.all_to_all(piled, "member", split_axis=0, concat_axis=0, tiled=True)
    term_across, term_beside, term_own, grad_score, slope = call(
        backward_kernel,
        [
            shaped(block, channels),
            shaped(block, channels),
            shaped(block, channels),
            shaped(PAIRS, slots, 2 * points),
            shaped(points, 128),
        ],
        [
            pltpu.VMEM((slots, 2 * channels), BF16),
            pltpu.VMEM((128, points), F32),
            pltpu.VMEM((ROWS, points), F32),
            pltpu.VMEM((slots, channels), BF16),
            pltpu.VMEM((HEADS * slots, points), F32),
        ],
        (
            info, piled, mine, analysis_t, scale_t, joint_t, query_halves, value_joint, weight,
            weight_16, slant, keyval_weight, keep,
        ),
        6,
        1_500_000_000,
        8_000_000,
        [SMEM],
    )
    from_beside = swap_beside(term_beside)
    from_across = swap_across(term_across)
    grad_grid, penalty = call(
        finish_kernel,
        [shaped(points, channels), shaped(points // members, variables, dtype=F32)],
        [
            pltpu.VMEM((points, channels), BF16),
            pltpu.VMEM((ROWS, points), F32),
            pltpu.VMEM((128, 128), F32),
        ],
        (
            info, keyval, grad_score, query_weight, slope, channels_t, piled, analysis_t, scale_t,
        ),
        4,
        400_000_000,
        4_000_000,
        [SMEM],
    )
    grad_nodes = term_own.astype(F32) + from_across.astype(F32) + from_beside.astype(F32)
    return (grad_nodes.astype(BF16)[None], grad_grid[None], penalty)


def solution(mesh):
    return jax.shard_map(
        per_device,
        mesh=mesh,
        in_specs=(
            P("member", "space", None),
            P("member", "space", None),
            P("member", "space", None),
            P("space", None),
            P("space", None),
            P("space"),
            P(),
            P(),
            P(),
            P(),
            P(),
        ),
        out_specs=(
            P("member", "space", None),
            P("member", "space", None),
            P(("space", "member"), None),
        ),
        check_vma=False,
    )
```

```python
import jax
import jax.numpy as jnp
from jax import lax
from jax.experimental import pallas as pl
from jax.experimental.pallas import tpu as pltpu
from jax.sharding import PartitionSpec as P

HEADS = 16
PAIRS = HEADS // 2
SOFT_CAP = 30.0
SOFTENED_QUAD = 0.01
FAIR_ALPHA = 0.95
OBJECTIVE_WEIGHT = 64.0
ROWS = 112
CHUNK = 512

F32 = jnp.float32
BF16 = jnp.bfloat16
MIB = 1024 * 1024

NN = (((1,), (0,)), ((), ()))
NT = (((1,), (1,)), ((), ()))
TN = (((0,), (0,)), ((), ()))


def mm(a, b, dims=NN):
    return lax.dot_general(a, b, dims, preferred_element_type=F32)


def split(x):
    hi = x.astype(BF16)
    return hi, (x - hi.astype(F32)).astype(BF16)


def diagonal(top, bottom):
    zero = jnp.zeros_like(top)
    return jnp.concatenate(
        [jnp.concatenate([top, zero], 1), jnp.concatenate([zero, bottom], 1)], 0
    )


def quadrants(full):
    return jnp.concatenate([full[:64, :128], full[64:, 128:]], 0)


def lanes_kernel(keep):
    first = (lax.broadcasted_iota(jnp.int32, (128, 128), 1) < 64).astype(F32)
    keep[:128] = first.astype(BF16)
    keep[128:] = (1.0 - first).astype(BF16)


def prepare_kernel(
    lattice, query_weight, channels_t, condition_t, query, query_hi, query_lo, base_t
):
    rows = lattice[...]
    for c in range(query_weight.shape[1] // CHUNK):
        at = slice(CHUNK * c, CHUNK * c + CHUNK)
        q = mm(rows, query_weight[:, at])
        query[:, at] = q.astype(BF16)
        hi, lo = split(q.T)
        query_hi[at, :] = hi
        query_lo[at, :] = lo
    variables = channels_t.shape[0]
    base_t[...] = jnp.zeros_like(base_t)
    base_t[:variables] = condition_t[:, 0, :] + mm(channels_t[...], rows, NT)


def attend_kernel(
    info, beside_late, across, beside_early, own, keyval_weight, query, query_hi, query_lo, edges_t, keep, area,
    variable,
    keyval, weight, weight_16, slant, mixture_t, query_halves, scale_t,
    nodes, score,
):
    block = own.shape[0]
    odd = info[1]
    nodes[block : 2 * block] = own[...]
    nodes[pl.ds(pl.multiple_of(odd * 2 * block, block), block)] = across[...]
    nodes[pl.ds(pl.multiple_of((1 - odd) * 2 * block, block), block)] = (
        beside_early[...] + beside_late[...]
    )
    slots, channels = nodes.shape
    points = edges_t.shape[1]
    x = nodes[...]
    for c in range(2 * channels // CHUNK):
        at = slice(CHUNK * c, CHUNK * c + CHUNK)
        keyval[:, at] = mm(x, keyval_weight[:, at]).astype(BF16)
    for p in range(PAIRS):
        at = slice(128 * p, 128 * p + 128)
        k = keyval[:, at]
        q_hi = query_hi[at, :]
        q_lo = query_lo[at, :]
        score[p] = mm(
            jnp.concatenate([k, k], 1),
            jnp.concatenate([diagonal(q_hi[:64], q_hi[64:]), diagonal(q_lo[:64], q_lo[64:])], 0),
        )
    number = lax.broadcasted_iota(jnp.int32, (slots, points), 0)
    count = jnp.zeros((slots, points), F32)
    for e in range(edges_t.shape[0]):
        count = count + (number == edges_t[e : e + 1, :]).astype(F32)
    count = jnp.concatenate([count, count], 1)
    for p in range(PAIRS):
        bent = jnp.tanh(score[p] * (1.0 / (8.0 * SOFT_CAP)))
        exponent = jnp.exp(SOFT_CAP * bent) * count
        w = exponent * (1.0 / jnp.sum(exponent, axis=0, keepdims=True))
        weight[p] = w
        weight_16[p] = w.astype(BF16)
        slant[p] = w * ((1.0 - bent * bent) * 0.125)
    left = keep[:128]
    right = keep[128:]
    for p in range(PAIRS):
        at = slice(128 * p, 128 * p + 128)
        v = keyval[:, channels + 128 * p : channels + 128 * p + 128]
        mixture_t[at, :] = quadrants(mm(v, weight_16[p], TN)).astype(BF16)
        query_halves[p] = jnp.concatenate([query[:, at] * left, query[:, at] * right], 0)
    variables = variable.shape[1]
    spread = jnp.concatenate(
        [
            jnp.broadcast_to(variable[...], (128, variables)),
            jnp.zeros((128, 128 - variables), F32),
        ],
        1,
    )
    scale_t[...] = spread.T[:ROWS] * area[...]


def joint_kernel(output_weight, channels_t, joint_t):
    variables, channels = channels_t.shape
    both = mm(channels_t[...], output_weight[...], NT)
    hi, lo = split(jnp.concatenate([both, jnp.zeros((ROWS - variables, channels), F32)], 0))
    joint_t[:ROWS] = hi
    joint_t[ROWS:] = lo


def forecast_kernel(joint_t, base_t, mixture_t, keyval, keep, piled, mine, value_joint):
    channels = mixture_t.shape[0]
    parts = mm(joint_t[...], mixture_t[...])
    forecast = (base_t[...] + (parts[:ROWS] + parts[ROWS:])).astype(BF16)
    mine[...] = forecast
    for m in range(piled.shape[0]):
        piled[m] = forecast
    slots = keyval.shape[0]
    pad = jnp.zeros((slots, 128 - ROWS), BF16)
    for p in range(PAIRS):
        at = slice(128 * p, 128 * p + 128)
        v = keyval[:, channels + 128 * p : channels + 128 * p + 128]
        hi = joint_t[:ROWS, at]
        lo = joint_t[ROWS:, at]
        for half in range(2):
            side = keep[128 * half : 128 * half + ROWS]
            high, low = split(
                mm(
                    jnp.concatenate([v, v], 1),
                    jnp.concatenate([hi * side, lo * side], 1),
                    NT,
                )
            )
            rows = slice((2 * p + half) * slots, (2 * p + half + 1) * slots)
            value_joint[rows, :] = jnp.concatenate([high, pad, low, pad], 1)


def backward_kernel(
    info, piled, mine, analysis_t, scale_t, joint_t, query_halves, value_joint, weight, weight_16,
    slant, keyval_weight, keep,
    term_across, term_beside, term_own, grad_score, slope,
    partial, slope_t, truth, terms, grad_weight,
):
    members = piled.shape[0]
    fair_eps = (1.0 - FAIR_ALPHA) / members
    variables = analysis_t.shape[0]
    truth[...] = jnp.zeros_like(truth)
    truth[:variables] = analysis_t[...]

    def bend(d):
        return d * lax.rsqrt(d * d + SOFTENED_QUAD)

    slope_t[ROWS:] = jnp.zeros((128 - ROWS, slope_t.shape[1]), F32)
    for r in range(0, ROWS, 16):
        at = slice(r, r + 16)
        forecast = mine[at].astype(F32)
        spread = jnp.zeros_like(forecast)
        for k in range(members):
            spread = spread + bend(forecast - piled[k, at].astype(F32))
        slope_t[at] = (OBJECTIVE_WEIGHT * scale_t[at]) * (
            bend(forecast - truth[at]) * (1.0 / members)
            - ((1.0 - fair_eps) / (members * (members - 1))) * spread
        )
    s_t = slope_t[...]
    s = s_t.T.astype(BF16)
    s_t = s_t.astype(BF16)
    slope[...] = s
    channels = keyval_weight.shape[1] // 2
    slots = partial.shape[0]
    grad_weight[...] = mm(value_joint[...], jnp.concatenate([s_t, s_t], 0))
    left = keep[:128]
    right = keep[128:]
    gm = mm(s[:, :ROWS], joint_t[:ROWS]).astype(BF16)
    for p in range(PAIRS):
        at = slice(128 * p, 128 * p + 128)
        v_at = slice(channels + 128 * p, channels + 128 * p + 128)
        halves = jnp.concatenate([gm[:, at] * left, gm[:, at] * right], 0)
        partial[:, v_at] = mm(weight_16[p], halves).astype(BF16)
    for p in range(PAIRS):
        low = 2 * p * slots
        gw = jnp.concatenate(
            [grad_weight[low : low + slots], grad_weight[low + slots : low + 2 * slots]], 1
        )
        w = weight[p]
        grad_score[p] = (
            slant[p] * (gw - jnp.sum(w * gw, axis=0, keepdims=True))
        ).astype(BF16)
    for p in range(PAIRS):
        at = slice(128 * p, 128 * p + 128)
        partial[:, at] = mm(grad_score[p], query_halves[p]).astype(BF16)
    terms[...] = (
        mm(partial[:, channels:], keyval_weight[:, channels:], NT)
        + mm(partial[:, :channels], keyval_weight[:, :channels], NT)
    ).astype(BF16)
    block = term_own.shape[0]
    odd = info[1]
    term_own[...] = terms[block : 2 * block]
    term_across[...] = terms[pl.ds(pl.multiple_of(odd * 2 * block, block), block)]
    term_beside[...] = terms[pl.ds(pl.multiple_of((1 - odd) * 2 * block, block), block)]


def finish_kernel(
    info, keyval, grad_score, query_weight, slope, channels_t, piled, analysis_t, scale_t,
    term_own, from_beside,
    grad_grid, penalty, total,
    grad_query, truth, turned,
):
    total[...] = term_own[...].astype(F32) + from_beside[...].astype(F32)
    variables = channels_t.shape[0]
    for p in range(PAIRS):
        at = slice(128 * p, 128 * p + 128)
        grad_query[:, at] = quadrants(mm(keyval[:, at], grad_score[p], TN)).T.astype(BF16)
    hidden = mm(slope[:, :variables], channels_t[...])
    for c in range(query_weight.shape[0] // CHUNK):
        at = slice(CHUNK * c, CHUNK * c + CHUNK)
        grad_grid[:, at] = (
            mm(grad_query[...], query_weight[at, :], NT) + hidden[:, at]
        ).astype(BF16)
    members = piled.shape[0]
    fair_eps = (1.0 - FAIR_ALPHA) / members
    truth[...] = jnp.zeros_like(truth)
    truth[:variables] = analysis_t[...]

    def soft(d):
        square = d * d + SOFTENED_QUAD
        return square * lax.rsqrt(square)

    turned[ROWS:] = jnp.zeros((128 - ROWS, 128), F32)
    for r in range(0, ROWS, 16):
        at = slice(r, r + 16)
        casts = [piled[m, at].astype(F32) for m in range(members)]
        goal = truth[at]
        accuracy = jnp.zeros_like(goal)
        spread = jnp.zeros_like(goal)
        for a in range(members):
            accuracy = accuracy + soft(casts[a] - goal)
            for b in range(a + 1, members):
                spread = spread + soft(casts[a] - casts[b])
        turned[at] = scale_t[at] * (
            accuracy * (1.0 / members) - ((1.0 - fair_eps) / (members * (members - 1))) * spread
        )
    turned[...] = turned[...].T
    rows = penalty.shape[0]
    start = pl.multiple_of(info[0] * rows, rows)
    penalty[...] = turned[pl.ds(start, rows), :variables]


def shaped(*dims, dtype=BF16):
    return jax.ShapeDtypeStruct(dims, dtype)


VMEM = pl.BlockSpec(memory_space=pltpu.VMEM)
HBM = pl.BlockSpec(memory_space=pltpu.HBM)
SMEM = pl.BlockSpec(memory_space=pltpu.SMEM)


def call(kernel, outs, scratch, args, limit, flops, moved, specs):
    specs = list(specs) + [VMEM] * (len(args) - len(specs))
    return pl.pallas_call(
        kernel,
        out_shape=outs,
        in_specs=specs,
        out_specs=[VMEM] * len(outs),
        scratch_shapes=scratch,
        compiler_params=pltpu.CompilerParams(vmem_limit_bytes=limit * MIB),
        cost_estimate=pl.CostEstimate(flops=flops, bytes_accessed=moved, transcendentals=0),
    )(*args)


def swap_across(value):
    count = lax.axis_size("space")
    return lax.ppermute(
        value, "space", [(i, (i + 1) % count if i % 2 else (i - 1) % count) for i in range(count)]
    )


def swap_beside(value, part=None):
    count = lax.axis_size("space")
    half = count // 4 * 2
    chosen = {None: range(count), 0: range(half), 1: range(half, count)}[part]
    return lax.ppermute(value, "space", [(i, i ^ 1) for i in chosen])


def per_device(
    coarse_vertex_embedding,
    lattice_bypass_embedding,
    initial_condition,
    verifying_analysis,
    edge_index,
    area_weight,
    variable_weight,
    query_weight,
    keyval_weight,
    output_weight,
    output_channel_matrix,
):
    own = coarse_vertex_embedding[0]
    lattice = lattice_bypass_embedding[0]
    block, channels = own.shape
    points = lattice.shape[0]
    variables = variable_weight.shape[0]
    slots = 3 * block
    members = lax.axis_size("member")
    condition_t = jnp.transpose(initial_condition, (2, 0, 1))
    analysis_t = verifying_analysis.T
    edges_t = edge_index.T
    channels_t = output_channel_matrix.T
    info = jnp.stack([lax.axis_index("member"), lax.axis_index("space") % 2]).astype(jnp.int32)

    beside_early = swap_beside(own, 0)
    across = swap_across(own)
    (keep,) = call(lanes_kernel, [shaped(256, 128)], [], (), 1, 3_000_000_000, 12_000_000, [])
    own, keep = lax.optimization_barrier((own, keep))
    beside_late = swap_beside(own, 1)
    query, query_hi, query_lo, base_t = call(
        prepare_kernel,
        [
            shaped(points, channels),
            shaped(channels, points),
            shaped(channels, points),
            shaped(ROWS, points, dtype=F32),
        ],
        [],
        (lattice, query_weight, channels_t, condition_t),
        4,
        1_000_000,
        1_000_000,
        [],
    )
    (joint_t,) = call(
        joint_kernel,
        [shaped(2 * ROWS, channels)],
        [],
        (output_weight, channels_t),
        4,
        3_000_000_000,
        10_000_000,
        [],
    )
    keyval, weight, weight_16, slant, mixture_t, query_halves, scale_t = call(
        attend_kernel,
        [
            shaped(slots, 2 * channels),
            shaped(PAIRS, slots, 2 * points, dtype=F32),
            shaped(PAIRS, slots, 2 * points),
            shaped(PAIRS, slots, 2 * points, dtype=F32),
            shaped(channels, points),
            shaped(PAIRS, 256, 128),
            shaped(ROWS, points, dtype=F32),
        ],
        [
            pltpu.VMEM((slots, channels), BF16),
            pltpu.VMEM((PAIRS, slots, 2 * points), F32),
        ],
        (
            info, beside_late, across, beside_early, own, keyval_weight, query, query_hi, query_lo, edges_t, keep,
            area_weight[None], variable_weight[None],
        ),
        4,
        2_000_000_000,
        8_000_000,
        [SMEM],
    )
    piled, mine, value_joint = call(
        forecast_kernel,
        [
            shaped(members, ROWS, points),
            shaped(ROWS, points),
            shaped(HEADS * slots, 256),
        ],
        [],
        (joint_t, base_t, mixture_t, keyval, keep),
        4,
        500_000_000,
        4_000_000,
        [],
    )
    piled = lax.all_to_all(piled, "member", split_axis=0, concat_axis=0, tiled=True)
    term_across, term_beside, term_own, grad_score, slope = call(
        backward_kernel,
        [
            shaped(block, channels),
            shaped(block, channels),
            shaped(block, channels),
            shaped(PAIRS, slots, 2 * points),
            shaped(points, 128),
        ],
        [
            pltpu.VMEM((slots, 2 * channels), BF16),
            pltpu.VMEM((128, points), F32),
            pltpu.VMEM((ROWS, points), F32),
            pltpu.VMEM((slots, channels), BF16),
            pltpu.VMEM((HEADS * slots, points), F32),
        ],
        (
            info, piled, mine, analysis_t, scale_t, joint_t, query_halves, value_joint, weight,
            weight_16, slant, keyval_weight, keep,
        ),
        6,
        1_500_000_000,
        8_000_000,
        [SMEM],
    )
    from_beside = swap_beside(term_beside)
    from_across = swap_across(term_across)
    grad_grid, penalty, total = call(
        finish_kernel,
        [
            shaped(points, channels),
            shaped(points // members, variables, dtype=F32),
            shaped(block, channels, dtype=F32),
        ],
        [
            pltpu.VMEM((points, channels), BF16),
            pltpu.VMEM((ROWS, points), F32),
            pltpu.VMEM((128, 128), F32),
        ],
        (
            info, keyval, grad_score, query_weight, slope, channels_t, piled, analysis_t, scale_t,
            term_own, from_beside,
        ),
        4,
        400_000_000,
        4_000_000,
        [SMEM],
    )
    grad_nodes = total + from_across.astype(F32)
    return (grad_nodes.astype(BF16)[None], grad_grid[None], penalty)


def solution(mesh):
    return jax.shard_map(
        per_device,
        mesh=mesh,
        in_specs=(
            P("member", "space", None),
            P("member", "space", None),
            P("member", "space", None),
            P("space", None),
            P("space", None),
            P("space"),
            P(),
            P(),
            P(),
            P(),
            P(),
        ),
        out_specs=(
            P("member", "space", None),
            P("member", "space", None),
            P(("space", "member"), None),
        ),
        check_vma=False,
    )
```

```python
import jax
import jax.numpy as jnp
from jax import lax
from jax.experimental import pallas as pl
from jax.experimental.pallas import tpu as pltpu
from jax.sharding import PartitionSpec as P

HEADS = 16
PAIRS = HEADS // 2
SOFT_CAP = 30.0
SOFTENED_QUAD = 0.01
FAIR_ALPHA = 0.95
OBJECTIVE_WEIGHT = 64.0
ROWS = 112
CHUNK = 512

F32 = jnp.float32
BF16 = jnp.bfloat16
MIB = 1024 * 1024

NN = (((1,), (0,)), ((), ()))
NT = (((1,), (1,)), ((), ()))
TN = (((0,), (0,)), ((), ()))


def mm(a, b, dims=NN):
    return lax.dot_general(a, b, dims, preferred_element_type=F32)


def split(x):
    hi = x.astype(BF16)
    return hi, (x - hi.astype(F32)).astype(BF16)


def diagonal(top, bottom):
    zero = jnp.zeros_like(top)
    return jnp.concatenate(
        [jnp.concatenate([top, zero], 1), jnp.concatenate([zero, bottom], 1)], 0
    )


def quadrants(full):
    return jnp.concatenate([full[:64, :128], full[64:, 128:]], 0)


def lanes_kernel(keep):
    first = (lax.broadcasted_iota(jnp.int32, (128, 128), 1) < 64).astype(F32)
    keep[:128] = first.astype(BF16)
    keep[128:] = (1.0 - first).astype(BF16)


def prepare_kernel(
    lattice, query_weight, channels_t, condition_t, keep, area, variable,
    query_hi, query_lo, base_t, query_halves, scale_t,
):
    rows = lattice[...]
    left = keep[:128]
    right = keep[128:]
    for c in range(query_weight.shape[1] // CHUNK):
        at = slice(CHUNK * c, CHUNK * c + CHUNK)
        q = mm(rows, query_weight[:, at])
        hi, lo = split(q.T)
        query_hi[at, :] = hi
        query_lo[at, :] = lo
        rounded = q.astype(BF16)
        for p in range(CHUNK // 128):
            pair = rounded[:, 128 * p : 128 * p + 128]
            query_halves[c * (CHUNK // 128) + p] = jnp.concatenate([pair * left, pair * right], 0)
    variables = channels_t.shape[0]
    spread = jnp.concatenate(
        [
            jnp.broadcast_to(variable[...], (128, variables)),
            jnp.zeros((128, 128 - variables), F32),
        ],
        1,
    )
    scale_t[...] = spread.T[:ROWS] * area[...]
    base_t[...] = jnp.zeros_like(base_t)
    base_t[:variables] = condition_t[:, 0, :] + mm(channels_t[...], rows, NT)


def attend_kernel(
    info, beside_late, across, beside_early, own, keyval_weight, query_hi, query_lo, edges_t, keep, joint_t, base_t,
    piled, mine, keyval, weight, weight_16, slant, value_joint,
    nodes, score, mixture_t,
):
    block = own.shape[0]
    odd = info[1]
    nodes[block : 2 * block] = own[...]
    nodes[pl.ds(pl.multiple_of(odd * 2 * block, block), block)] = across[...]
    nodes[pl.ds(pl.multiple_of((1 - odd) * 2 * block, block), block)] = (
        beside_early[...] + beside_late[...]
    )
    slots, channels = nodes.shape
    points = edges_t.shape[1]
    x = nodes[...]
    for c in range(2 * channels // CHUNK):
        at = slice(CHUNK * c, CHUNK * c + CHUNK)
        keyval[:, at] = mm(x, keyval_weight[:, at]).astype(BF16)
    for p in range(PAIRS):
        at = slice(128 * p, 128 * p + 128)
        k = keyval[:, at]
        q_hi = query_hi[at, :]
        q_lo = query_lo[at, :]
        score[p] = mm(
            jnp.concatenate([k, k], 1),
            jnp.concatenate([diagonal(q_hi[:64], q_hi[64:]), diagonal(q_lo[:64], q_lo[64:])], 0),
        )
    number = lax.broadcasted_iota(jnp.int32, (slots, points), 0)
    count = jnp.zeros((slots, points), F32)
    for e in range(edges_t.shape[0]):
        count = count + (number == edges_t[e : e + 1, :]).astype(F32)
    count = jnp.concatenate([count, count], 1)
    for p in range(PAIRS):
        bent = jnp.tanh(score[p] * (1.0 / (8.0 * SOFT_CAP)))
        exponent = jnp.exp(SOFT_CAP * bent) * count
        w = exponent * (1.0 / jnp.sum(exponent, axis=0, keepdims=True))
        weight[p] = w
        weight_16[p] = w.astype(BF16)
        slant[p] = w * ((1.0 - bent * bent) * 0.125)
    for p in range(PAIRS):
        at = slice(128 * p, 128 * p + 128)
        v = keyval[:, channels + 128 * p : channels + 128 * p + 128]
        mixture_t[at, :] = quadrants(mm(v, weight_16[p], TN)).astype(BF16)
    parts = mm(joint_t[...], mixture_t[...])
    forecast = (base_t[...] + (parts[:ROWS] + parts[ROWS:])).astype(BF16)
    mine[...] = forecast
    for m in range(piled.shape[0]):
        piled[m] = forecast
    pad = jnp.zeros((slots, 128 - ROWS), BF16)
    for p in range(PAIRS):
        at = slice(128 * p, 128 * p + 128)
        v = keyval[:, channels + 128 * p : channels + 128 * p + 128]
        hi = joint_t[:ROWS, at]
        lo = joint_t[ROWS:, at]
        for half in range(2):
            side = keep[128 * half : 128 * half + ROWS]
            high, low = split(
                mm(
                    jnp.concatenate([v, v], 1),
                    jnp.concatenate([hi * side, lo * side], 1),
                    NT,
                )
            )
            rows = slice((2 * p + half) * slots, (2 * p + half + 1) * slots)
            value_joint[rows, :] = jnp.concatenate([high, pad, low, pad], 1)


def joint_kernel(output_weight, channels_t, joint_t):
    variables, channels = channels_t.shape
    both = mm(channels_t[...], output_weight[...], NT)
    hi, lo = split(jnp.concatenate([both, jnp.zeros((ROWS - variables, channels), F32)], 0))
    joint_t[:ROWS] = hi
    joint_t[ROWS:] = lo


def backward_kernel(
    info, piled, mine, analysis_t, scale_t, joint_t, query_halves, value_joint, weight, weight_16,
    slant, keyval_weight, keep,
    term_across, term_beside, term_own, grad_score, slope,
    partial, slope_t, truth, terms, grad_weight,
):
    members = piled.shape[0]
    fair_eps = (1.0 - FAIR_ALPHA) / members
    variables = analysis_t.shape[0]
    truth[...] = jnp.zeros_like(truth)
    truth[:variables] = analysis_t[...]

    def bend(d):
        return d * lax.rsqrt(d * d + SOFTENED_QUAD)

    slope_t[ROWS:] = jnp.zeros((128 - ROWS, slope_t.shape[1]), F32)
    for r in range(0, ROWS, 16):
        at = slice(r, r + 16)
        forecast = mine[at].astype(F32)
        spread = jnp.zeros_like(forecast)
        for k in range(members):
            spread = spread + bend(forecast - piled[k, at].astype(F32))
        slope_t[at] = (OBJECTIVE_WEIGHT * scale_t[at]) * (
            bend(forecast - truth[at]) * (1.0 / members)
            - ((1.0 - fair_eps) / (members * (members - 1))) * spread
        )
    s_t = slope_t[...]
    s = s_t.T.astype(BF16)
    s_t = s_t.astype(BF16)
    slope[...] = s
    channels = keyval_weight.shape[1] // 2
    slots = partial.shape[0]
    grad_weight[...] = mm(value_joint[...], jnp.concatenate([s_t, s_t], 0))
    left = keep[:128]
    right = keep[128:]
    gm = mm(s[:, :ROWS], joint_t[:ROWS]).astype(BF16)
    for p in range(PAIRS):
        at = slice(128 * p, 128 * p + 128)
        v_at = slice(channels + 128 * p, channels + 128 * p + 128)
        halves = jnp.concatenate([gm[:, at] * left, gm[:, at] * right], 0)
        partial[:, v_at] = mm(weight_16[p], halves).astype(BF16)
    for p in range(PAIRS):
        low = 2 * p * slots
        gw = jnp.concatenate(
            [grad_weight[low : low + slots], grad_weight[low + slots : low + 2 * slots]], 1
        )
        w = weight[p]
        grad_score[p] = (
            slant[p] * (gw - jnp.sum(w * gw, axis=0, keepdims=True))
        ).astype(BF16)
    for p in range(PAIRS):
        at = slice(128 * p, 128 * p + 128)
        partial[:, at] = mm(grad_score[p], query_halves[p]).astype(BF16)
    terms[...] = (
        mm(partial[:, channels:], keyval_weight[:, channels:], NT)
        + mm(partial[:, :channels], keyval_weight[:, :channels], NT)
    ).astype(BF16)
    block = term_own.shape[0]
    odd = info[1]
    term_own[...] = terms[block : 2 * block]
    term_across[...] = terms[pl.ds(pl.multiple_of(odd * 2 * block, block), block)]
    term_beside[...] = terms[pl.ds(pl.multiple_of((1 - odd) * 2 * block, block), block)]


def finish_kernel(
    info, keyval, grad_score, query_weight, slope, channels_t, piled, analysis_t, scale_t,
    term_own, from_beside,
    grad_grid, penalty, total,
    grad_query, truth, turned,
):
    total[...] = term_own[...].astype(F32) + from_beside[...].astype(F32)
    variables = channels_t.shape[0]
    for p in range(PAIRS):
        at = slice(128 * p, 128 * p + 128)
        grad_query[:, at] = quadrants(mm(keyval[:, at], grad_score[p], TN)).T.astype(BF16)
    hidden = mm(slope[:, :variables], channels_t[...])
    for c in range(query_weight.shape[0] // CHUNK):
        at = slice(CHUNK * c, CHUNK * c + CHUNK)
        grad_grid[:, at] = (
            mm(grad_query[...], query_weight[at, :], NT) + hidden[:, at]
        ).astype(BF16)
    members = piled.shape[0]
    fair_eps = (1.0 - FAIR_ALPHA) / members
    truth[...] = jnp.zeros_like(truth)
    truth[:variables] = analysis_t[...]

    def soft(d):
        square = d * d + SOFTENED_QUAD
        return square * lax.rsqrt(square)

    turned[ROWS:] = jnp.zeros((128 - ROWS, 128), F32)
    for r in range(0, ROWS, 16):
        at = slice(r, r + 16)
        casts = [piled[m, at].astype(F32) for m in range(members)]
        goal = truth[at]
        accuracy = jnp.zeros_like(goal)
        spread = jnp.zeros_like(goal)
        for a in range(members):
            accuracy = accuracy + soft(casts[a] - goal)
            for b in range(a + 1, members):
                spread = spread + soft(casts[a] - casts[b])
        turned[at] = scale_t[at] * (
            accuracy * (1.0 / members) - ((1.0 - fair_eps) / (members * (members - 1))) * spread
        )
    turned[...] = turned[...].T
    rows = penalty.shape[0]
    start = pl.multiple_of(info[0] * rows, rows)
    penalty[...] = turned[pl.ds(start, rows), :variables]


def shaped(*dims, dtype=BF16):
    return jax.ShapeDtypeStruct(dims, dtype)


VMEM = pl.BlockSpec(memory_space=pltpu.VMEM)
HBM = pl.BlockSpec(memory_space=pltpu.HBM)
SMEM = pl.BlockSpec(memory_space=pltpu.SMEM)


def call(kernel, outs, scratch, args, limit, flops, moved, specs):
    specs = list(specs) + [VMEM] * (len(args) - len(specs))
    return pl.pallas_call(
        kernel,
        out_shape=outs,
        in_specs=specs,
        out_specs=[VMEM] * len(outs),
        scratch_shapes=scratch,
        compiler_params=pltpu.CompilerParams(vmem_limit_bytes=limit * MIB),
        cost_estimate=pl.CostEstimate(flops=flops, bytes_accessed=moved, transcendentals=0),
    )(*args)


def swap_across(value):
    count = lax.axis_size("space")
    return lax.ppermute(
        value, "space", [(i, (i + 1) % count if i % 2 else (i - 1) % count) for i in range(count)]
    )


def swap_beside(value, part):
    count = lax.axis_size("space")
    half = count // 4 * 2
    chosen = (range(half), range(half, count))[part]
    return lax.ppermute(value, "space", [(i, i ^ 1) for i in chosen])


def per_device(
    coarse_vertex_embedding,
    lattice_bypass_embedding,
    initial_condition,
    verifying_analysis,
    edge_index,
    area_weight,
    variable_weight,
    query_weight,
    keyval_weight,
    output_weight,
    output_channel_matrix,
):
    own = coarse_vertex_embedding[0]
    lattice = lattice_bypass_embedding[0]
    block, channels = own.shape
    points = lattice.shape[0]
    variables = variable_weight.shape[0]
    slots = 3 * block
    members = lax.axis_size("member")
    condition_t = jnp.transpose(initial_condition, (2, 0, 1))
    analysis_t = verifying_analysis.T
    edges_t = edge_index.T
    channels_t = output_channel_matrix.T
    info = jnp.stack([lax.axis_index("member"), lax.axis_index("space") % 2]).astype(jnp.int32)

    beside_early = swap_beside(own, 0)
    across = swap_across(own)
    (keep,) = call(lanes_kernel, [shaped(256, 128)], [], (), 1, 3_000_000_000, 12_000_000, [])
    own, keep = lax.optimization_barrier((own, keep))
    beside_late = swap_beside(own, 1)
    query_hi, query_lo, base_t, query_halves, scale_t = call(
        prepare_kernel,
        [
            shaped(channels, points),
            shaped(channels, points),
            shaped(ROWS, points, dtype=F32),
            shaped(PAIRS, 256, 128),
            shaped(ROWS, points, dtype=F32),
        ],
        [],
        (
            lattice, query_weight, channels_t, condition_t, keep, area_weight[None],
            variable_weight[None],
        ),
        4,
        1_000_000,
        1_000_000,
        [],
    )
    (joint_t,) = call(
        joint_kernel,
        [shaped(2 * ROWS, channels)],
        [],
        (output_weight, channels_t),
        4,
        3_000_000_000,
        10_000_000,
        [],
    )
    piled, mine, keyval, weight, weight_16, slant, value_joint = call(
        attend_kernel,
        [
            shaped(members, ROWS, points),
            shaped(ROWS, points),
            shaped(slots, 2 * channels),
            shaped(PAIRS, slots, 2 * points, dtype=F32),
            shaped(PAIRS, slots, 2 * points),
            shaped(PAIRS, slots, 2 * points, dtype=F32),
            shaped(HEADS * slots, 256),
        ],
        [
            pltpu.VMEM((slots, channels), BF16),
            pltpu.VMEM((PAIRS, slots, 2 * points), F32),
            pltpu.VMEM((channels, points), BF16),
        ],
        (
            info, beside_late, across, beside_early, own, keyval_weight, query_hi, query_lo,
            edges_t, keep, joint_t, base_t,
        ),
        4,
        2_000_000_000,
        8_000_000,
        [SMEM],
    )
    piled = lax.all_to_all(piled, "member", split_axis=0, concat_axis=0, tiled=True)
    term_across, term_beside, term_own, grad_score, slope = call(
        backward_kernel,
        [
            shaped(block, channels),
            shaped(block, channels),
            shaped(block, channels),
            shaped(PAIRS, slots, 2 * points),
            shaped(points, 128),
        ],
        [
            pltpu.VMEM((slots, 2 * channels), BF16),
            pltpu.VMEM((128, points), F32),
            pltpu.VMEM((ROWS, points), F32),
            pltpu.VMEM((slots, channels), BF16),
            pltpu.VMEM((HEADS * slots, points), F32),
        ],
        (
            info, piled, mine, analysis_t, scale_t, joint_t, query_halves, value_joint, weight,
            weight_16, slant, keyval_weight, keep,
        ),
        6,
        1_500_000_000,
        8_000_000,
        [SMEM],
    )
    from_beside = swap_beside(term_beside, 0)
    from_late = swap_beside(term_beside, 1)
    from_across = swap_across(term_across)
    grad_grid, penalty, total = call(
        finish_kernel,
        [
            shaped(points, channels),
            shaped(points // members, variables, dtype=F32),
            shaped(block, channels, dtype=F32),
        ],
        [
            pltpu.VMEM((points, channels), BF16),
            pltpu.VMEM((ROWS, points), F32),
            pltpu.VMEM((128, 128), F32),
        ],
        (
            info, keyval, grad_score, query_weight, slope, channels_t, piled, analysis_t, scale_t,
            term_own, from_beside,
        ),
        4,
        400_000_000,
        4_000_000,
        [SMEM],
    )
    grad_nodes = total + from_across.astype(F32) + from_late.astype(F32)
    return (grad_nodes.astype(BF16)[None], grad_grid[None], penalty)


def solution(mesh):
    return jax.shard_map(
        per_device,
        mesh=mesh,
        in_specs=(
            P("member", "space", None),
            P("member", "space", None),
            P("member", "space", None),
            P("space", None),
            P("space", None),
            P("space"),
            P(),
            P(),
            P(),
            P(),
            P(),
        ),
        out_specs=(
            P("member", "space", None),
            P("member", "space", None),
            P(("space", "member"), None),
        ),
        check_vma=False,
    )
```

```python
import jax
import jax.numpy as jnp
from jax import lax
from jax.experimental import pallas as pl
from jax.experimental.pallas import tpu as pltpu
from jax.sharding import PartitionSpec as P

HEADS = 16
PAIRS = HEADS // 2
SOFT_CAP = 30.0
SOFTENED_QUAD = 0.01
FAIR_ALPHA = 0.95
OBJECTIVE_WEIGHT = 64.0
ROWS = 112
SENT = 104
CHUNK = 512

F32 = jnp.float32
BF16 = jnp.bfloat16
MIB = 1024 * 1024

NN = (((1,), (0,)), ((), ()))
NT = (((1,), (1,)), ((), ()))
TN = (((0,), (0,)), ((), ()))


def mm(a, b, dims=NN):
    return lax.dot_general(a, b, dims, preferred_element_type=F32)


def split(x):
    hi = x.astype(BF16)
    return hi, (x - hi.astype(F32)).astype(BF16)


def diagonal(top, bottom):
    zero = jnp.zeros_like(top)
    return jnp.concatenate(
        [jnp.concatenate([top, zero], 1), jnp.concatenate([zero, bottom], 1)], 0
    )


def quadrants(full):
    return jnp.concatenate([full[:64, :128], full[64:, 128:]], 0)


def lanes_kernel(keep):
    first = (lax.broadcasted_iota(jnp.int32, (128, 128), 1) < 64).astype(F32)
    keep[:128] = first.astype(BF16)
    keep[128:] = (1.0 - first).astype(BF16)


def prepare_kernel(
    lattice, query_weight, channels_t, condition_t, query, query_hi, query_lo, base_t
):
    rows = lattice[...]
    for c in range(query_weight.shape[1] // CHUNK):
        at = slice(CHUNK * c, CHUNK * c + CHUNK)
        q = mm(rows, query_weight[:, at])
        query[:, at] = q.astype(BF16)
        hi, lo = split(q.T)
        query_hi[at, :] = hi
        query_lo[at, :] = lo
    variables = channels_t.shape[0]
    base_t[...] = jnp.zeros_like(base_t)
    base_t[:variables] = condition_t[:, 0, :] + mm(channels_t[...], rows, NT)


def attend_kernel(
    info, beside_late, across, beside_early, own, keyval_weight, query, query_hi, query_lo, edges_t, keep, area,
    variable,
    keyval, weight, weight_16, slant, mixture_t, query_halves, scale_t,
    nodes, score,
):
    block = own.shape[0]
    odd = info[1]
    nodes[block : 2 * block] = own[...]
    nodes[pl.ds(pl.multiple_of(odd * 2 * block, block), block)] = across[...]
    nodes[pl.ds(pl.multiple_of((1 - odd) * 2 * block, block), block)] = (
        beside_early[...] + beside_late[...]
    )
    slots, channels = nodes.shape
    points = edges_t.shape[1]
    x = nodes[...]
    for c in range(2 * channels // CHUNK):
        at = slice(CHUNK * c, CHUNK * c + CHUNK)
        keyval[:, at] = mm(x, keyval_weight[:, at]).astype(BF16)
    for p in range(PAIRS):
        at = slice(128 * p, 128 * p + 128)
        k = keyval[:, at]
        q_hi = query_hi[at, :]
        q_lo = query_lo[at, :]
        score[p] = mm(
            jnp.concatenate([k, k], 1),
            jnp.concatenate([diagonal(q_hi[:64], q_hi[64:]), diagonal(q_lo[:64], q_lo[64:])], 0),
        )
    number = lax.broadcasted_iota(jnp.int32, (slots, points), 0)
    count = jnp.zeros((slots, points), F32)
    for e in range(edges_t.shape[0]):
        count = count + (number == edges_t[e : e + 1, :]).astype(F32)
    count = jnp.concatenate([count, count], 1)
    for p in range(PAIRS):
        bent = jnp.tanh(score[p] * (1.0 / (8.0 * SOFT_CAP)))
        exponent = jnp.exp(SOFT_CAP * bent) * count
        w = exponent * (1.0 / jnp.sum(exponent, axis=0, keepdims=True))
        weight[p] = w
        weight_16[p] = w.astype(BF16)
        slant[p] = w * ((1.0 - bent * bent) * 0.125)
    left = keep[:128]
    right = keep[128:]
    for p in range(PAIRS):
        at = slice(128 * p, 128 * p + 128)
        v = keyval[:, channels + 128 * p : channels + 128 * p + 128]
        mixture_t[at, :] = quadrants(mm(v, weight_16[p], TN)).astype(BF16)
        query_halves[p] = jnp.concatenate([query[:, at] * left, query[:, at] * right], 0)
    variables = variable.shape[1]
    spread = jnp.concatenate(
        [
            jnp.broadcast_to(variable[...], (128, variables)),
            jnp.zeros((128, 128 - variables), F32),
        ],
        1,
    )
    scale_t[...] = spread.T[:ROWS] * area[...]


def joint_kernel(output_weight, channels_t, joint_t):
    variables, channels = channels_t.shape
    both = mm(channels_t[...], output_weight[...], NT)
    hi, lo = split(jnp.concatenate([both, jnp.zeros((ROWS - variables, channels), F32)], 0))
    joint_t[:ROWS] = hi
    joint_t[ROWS:] = lo


def forecast_kernel(joint_t, base_t, mixture_t, keyval, keep, piled, mine, value_joint):
    channels = mixture_t.shape[0]
    parts = mm(joint_t[...], mixture_t[...])
    forecast = (base_t[...] + (parts[:ROWS] + parts[ROWS:])).astype(BF16)
    mine[...] = forecast
    for m in range(piled.shape[0]):
        piled[m] = forecast[:SENT]
    slots = keyval.shape[0]
    pad = jnp.zeros((slots, 128 - ROWS), BF16)
    for p in range(PAIRS):
        at = slice(128 * p, 128 * p + 128)
        v = keyval[:, channels + 128 * p : channels + 128 * p + 128]
        hi = joint_t[:ROWS, at]
        lo = joint_t[ROWS:, at]
        for half in range(2):
            side = keep[128 * half : 128 * half + ROWS]
            high, low = split(
                mm(
                    jnp.concatenate([v, v], 1),
                    jnp.concatenate([hi * side, lo * side], 1),
                    NT,
                )
            )
            rows = slice((2 * p + half) * slots, (2 * p + half + 1) * slots)
            value_joint[rows, :] = jnp.concatenate([high, pad, low, pad], 1)


def widen(piled, wide):
    for m in range(piled.shape[0]):
        wide[m, :SENT] = piled[m].astype(F32)
        wide[m, SENT:] = jnp.zeros((ROWS - SENT, wide.shape[2]), F32)


def backward_kernel(
    info, piled, mine, analysis_t, scale_t, joint_t, query_halves, value_joint, weight, weight_16,
    slant, keyval_weight, keep,
    term_across, term_beside, term_own, grad_score, slope,
    partial, slope_t, truth, terms, grad_weight, wide,
):
    widen(piled, wide)
    members = piled.shape[0]
    fair_eps = (1.0 - FAIR_ALPHA) / members
    variables = analysis_t.shape[0]
    truth[...] = jnp.zeros_like(truth)
    truth[:variables] = analysis_t[...]

    def bend(d):
        return d * lax.rsqrt(d * d + SOFTENED_QUAD)

    slope_t[ROWS:] = jnp.zeros((128 - ROWS, slope_t.shape[1]), F32)
    for r in range(0, ROWS, 16):
        at = slice(r, r + 16)
        forecast = mine[at].astype(F32)
        spread = jnp.zeros_like(forecast)
        for k in range(members):
            spread = spread + bend(forecast - wide[k, at])
        slope_t[at] = (OBJECTIVE_WEIGHT * scale_t[at]) * (
            bend(forecast - truth[at]) * (1.0 / members)
            - ((1.0 - fair_eps) / (members * (members - 1))) * spread
        )
    s_t = slope_t[...]
    s = s_t.T.astype(BF16)
    s_t = s_t.astype(BF16)
    slope[...] = s
    channels = keyval_weight.shape[1] // 2
    slots = partial.shape[0]
    grad_weight[...] = mm(value_joint[...], jnp.concatenate([s_t, s_t], 0))
    left = keep[:128]
    right = keep[128:]
    gm = mm(s[:, :ROWS], joint_t[:ROWS]).astype(BF16)
    for p in range(PAIRS):
        at = slice(128 * p, 128 * p + 128)
        v_at = slice(channels + 128 * p, channels + 128 * p + 128)
        halves = jnp.concatenate([gm[:, at] * left, gm[:, at] * right], 0)
        partial[:, v_at] = mm(weight_16[p], halves).astype(BF16)
    for p in range(PAIRS):
        low = 2 * p * slots
        gw = jnp.concatenate(
            [grad_weight[low : low + slots], grad_weight[low + slots : low + 2 * slots]], 1
        )
        w = weight[p]
        grad_score[p] = (
            slant[p] * (gw - jnp.sum(w * gw, axis=0, keepdims=True))
        ).astype(BF16)
    for p in range(PAIRS):
        at = slice(128 * p, 128 * p + 128)
        partial[:, at] = mm(grad_score[p], query_halves[p]).astype(BF16)
    terms[...] = (
        mm(partial[:, channels:], keyval_weight[:, channels:], NT)
        + mm(partial[:, :channels], keyval_weight[:, :channels], NT)
    ).astype(BF16)
    block = term_own.shape[0]
    odd = info[1]
    term_own[...] = terms[block : 2 * block]
    term_across[...] = terms[pl.ds(pl.multiple_of(odd * 2 * block, block), block)]
    term_beside[...] = terms[pl.ds(pl.multiple_of((1 - odd) * 2 * block, block), block)]


def finish_kernel(
    info, keyval, grad_score, query_weight, slope, channels_t, piled, analysis_t, scale_t,
    term_own, from_beside,
    grad_grid, penalty, total,
    grad_query, truth, turned, wide,
):
    widen(piled, wide)
    total[...] = term_own[...].astype(F32) + from_beside[...].astype(F32)
    variables = channels_t.shape[0]
    for p in range(PAIRS):
        at = slice(128 * p, 128 * p + 128)
        grad_query[:, at] = quadrants(mm(keyval[:, at], grad_score[p], TN)).T.astype(BF16)
    hidden = mm(slope[:, :variables], channels_t[...])
    for c in range(query_weight.shape[0] // CHUNK):
        at = slice(CHUNK * c, CHUNK * c + CHUNK)
        grad_grid[:, at] = (
            mm(grad_query[...], query_weight[at, :], NT) + hidden[:, at]
        ).astype(BF16)
    members = piled.shape[0]
    fair_eps = (1.0 - FAIR_ALPHA) / members
    truth[...] = jnp.zeros_like(truth)
    truth[:variables] = analysis_t[...]

    def soft(d):
        square = d * d + SOFTENED_QUAD
        return square * lax.rsqrt(square)

    turned[ROWS:] = jnp.zeros((128 - ROWS, 128), F32)
    for r in range(0, ROWS, 16):
        at = slice(r, r + 16)
        casts = [wide[m, at] for m in range(members)]
        goal = truth[at]
        accuracy = jnp.zeros_like(goal)
        spread = jnp.zeros_like(goal)
        for a in range(members):
            accuracy = accuracy + soft(casts[a] - goal)
            for b in range(a + 1, members):
                spread = spread + soft(casts[a] - casts[b])
        turned[at] = scale_t[at] * (
            accuracy * (1.0 / members) - ((1.0 - fair_eps) / (members * (members - 1))) * spread
        )
    turned[...] = turned[...].T
    rows = penalty.shape[0]
    start = pl.multiple_of(info[0] * rows, rows)
    penalty[...] = turned[pl.ds(start, rows), :variables]


def shaped(*dims, dtype=BF16):
    return jax.ShapeDtypeStruct(dims, dtype)


VMEM = pl.BlockSpec(memory_space=pltpu.VMEM)
HBM = pl.BlockSpec(memory_space=pltpu.HBM)
SMEM = pl.BlockSpec(memory_space=pltpu.SMEM)


def call(kernel, outs, scratch, args, limit, flops, moved, specs):
    specs = list(specs) + [VMEM] * (len(args) - len(specs))
    return pl.pallas_call(
        kernel,
        out_shape=outs,
        in_specs=specs,
        out_specs=[VMEM] * len(outs),
        scratch_shapes=scratch,
        compiler_params=pltpu.CompilerParams(vmem_limit_bytes=limit * MIB),
        cost_estimate=pl.CostEstimate(flops=flops, bytes_accessed=moved, transcendentals=0),
    )(*args)


def swap_across(value):
    count = lax.axis_size("space")
    return lax.ppermute(
        value, "space", [(i, (i + 1) % count if i % 2 else (i - 1) % count) for i in range(count)]
    )


def swap_beside(value, part=None):
    count = lax.axis_size("space")
    half = count // 4 * 2
    chosen = {None: range(count), 0: range(half), 1: range(half, count)}[part]
    return lax.ppermute(value, "space", [(i, i ^ 1) for i in chosen])


def per_device(
    coarse_vertex_embedding,
    lattice_bypass_embedding,
    initial_condition,
    verifying_analysis,
    edge_index,
    area_weight,
    variable_weight,
    query_weight,
    keyval_weight,
    output_weight,
    output_channel_matrix,
):
    own = coarse_vertex_embedding[0]
    lattice = lattice_bypass_embedding[0]
    block, channels = own.shape
    points = lattice.shape[0]
    variables = variable_weight.shape[0]
    slots = 3 * block
    members = lax.axis_size("member")
    condition_t = jnp.transpose(initial_condition, (2, 0, 1))
    analysis_t = verifying_analysis.T
    edges_t = edge_index.T
    channels_t = output_channel_matrix.T
    info = jnp.stack([lax.axis_index("member"), lax.axis_index("space") % 2]).astype(jnp.int32)

    beside_early = swap_beside(own, 0)
    across = swap_across(own)
    (keep,) = call(lanes_kernel, [shaped(256, 128)], [], (), 1, 3_000_000_000, 12_000_000, [])
    own, keep = lax.optimization_barrier((own, keep))
    beside_late = swap_beside(own, 1)
    query, query_hi, query_lo, base_t = call(
        prepare_kernel,
        [
            shaped(points, channels),
            shaped(channels, points),
            shaped(channels, points),
            shaped(ROWS, points, dtype=F32),
        ],
        [],
        (lattice, query_weight, channels_t, condition_t),
        4,
        1_000_000,
        1_000_000,
        [],
    )
    (joint_t,) = call(
        joint_kernel,
        [shaped(2 * ROWS, channels)],
        [],
        (output_weight, channels_t),
        4,
        3_000_000_000,
        10_000_000,
        [],
    )
    keyval, weight, weight_16, slant, mixture_t, query_halves, scale_t = call(
        attend_kernel,
        [
            shaped(slots, 2 * channels),
            shaped(PAIRS, slots, 2 * points, dtype=F32),
            shaped(PAIRS, slots, 2 * points),
            shaped(PAIRS, slots, 2 * points, dtype=F32),
            shaped(channels, points),
            shaped(PAIRS, 256, 128),
            shaped(ROWS, points, dtype=F32),
        ],
        [
            pltpu.VMEM((slots, channels), BF16),
            pltpu.VMEM((PAIRS, slots, 2 * points), F32),
        ],
        (
            info, beside_late, across, beside_early, own, keyval_weight, query, query_hi, query_lo, edges_t, keep,
            area_weight[None], variable_weight[None],
        ),
        4,
        2_000_000_000,
        8_000_000,
        [SMEM],
    )
    piled, mine, value_joint = call(
        forecast_kernel,
        [
            shaped(members, SENT, points),
            shaped(ROWS, points),
            shaped(HEADS * slots, 256),
        ],
        [],
        (joint_t, base_t, mixture_t, keyval, keep),
        4,
        500_000_000,
        4_000_000,
        [],
    )
    piled = lax.all_to_all(piled, "member", split_axis=0, concat_axis=0, tiled=True)
    term_across, term_beside, term_own, grad_score, slope = call(
        backward_kernel,
        [
            shaped(block, channels),
            shaped(block, channels),
            shaped(block, channels),
            shaped(PAIRS, slots, 2 * points),
            shaped(points, 128),
        ],
        [
            pltpu.VMEM((slots, 2 * channels), BF16),
            pltpu.VMEM((128, points), F32),
            pltpu.VMEM((ROWS, points), F32),
            pltpu.VMEM((slots, channels), BF16),
            pltpu.VMEM((HEADS * slots, points), F32),
            pltpu.VMEM((members, ROWS, points), F32),
        ],
        (
            info, piled, mine, analysis_t, scale_t, joint_t, query_halves, value_joint, weight,
            weight_16, slant, keyval_weight, keep,
        ),
        6,
        1_500_000_000,
        8_000_000,
        [SMEM],
    )
    from_beside = swap_beside(term_beside)
    from_across = swap_across(term_across)
    grad_grid, penalty, total = call(
        finish_kernel,
        [
            shaped(points, channels),
            shaped(points // members, variables, dtype=F32),
            shaped(block, channels, dtype=F32),
        ],
        [
            pltpu.VMEM((points, channels), BF16),
            pltpu.VMEM((ROWS, points), F32),
            pltpu.VMEM((128, 128), F32),
            pltpu.VMEM((members, ROWS, points), F32),
        ],
        (
            info, keyval, grad_score, query_weight, slope, channels_t, piled, analysis_t, scale_t,
            term_own, from_beside,
        ),
        4,
        400_000_000,
        4_000_000,
        [SMEM],
    )
    grad_nodes = total + from_across.astype(F32)
    return (grad_nodes.astype(BF16)[None], grad_grid[None], penalty)


def solution(mesh):
    return jax.shard_map(
        per_device,
        mesh=mesh,
        in_specs=(
            P("member", "space", None),
            P("member", "space", None),
            P("member", "space", None),
            P("space", None),
            P("space", None),
            P("space"),
            P(),
            P(),
            P(),
            P(),
            P(),
        ),
        out_specs=(
            P("member", "space", None),
            P("member", "space", None),
            P(("space", "member"), None),
        ),
        check_vma=False,
    )
```
